32 devices in a mesh: grp: 2 (over x), tm: 8 (over z, y), inp: 2 (over core).
Axes of the slice: x: 2, y: 2, z: 4, core: 2. Of those that a mesh axis runs over, the one named last changes fastest.
Arguments:
- samples: bfloat16 [256, 1024, 2048], P('grp', ('tm', 'inp')), parts along dimension 0, may hold values from -6 to 6
- filter_taps: float32 [8, 1024], replicated, may hold values from -2 to 2
- flagged: int32 [2048], P('grp'), parts along dimension 0, may hold values 0 or 1
- input_order: int32 [1024], replicated, may hold values from 0 to 1023, each once
Outputs:
- visibilities: bfloat16 [32, 1024, 2048], P(('grp', 'tm'), 'inp'), parts along dimension 0
The draws below stay inside these ranges and needn't reach their ends.
There are 2 independent parts, one for each index of `grp`. The reference program is written for one: setup_inputs(seed, part) draws one part's arguments, and reference() takes and returns one part's arrays. A program takes and returns all parts, laid end to end along the dimension named above; an argument that names none is the same for every part. Nothing has to cross between parts.
Inputs may be any that keep to these rules, and one draw needn't show every extreme that they name: `input_order`: each input appears at exactly one correlator position.
All inputs are finite; a program needn't handle non-finite values.
Results may differ from the reference program's by a relative error of at most 0.007.
Values may be sent and summed in bfloat16 or wider, within the bound.
A program may use at most 128 MiB of HBM per device.

```python
import math
import jax
import jax.numpy as jnp
from jax import lax

NIN = 1024
NCH = 1024
TAPS = 8
FRAMES = 128
CHANS = 16


def touch_ends(array, key, least, top_value):
    spot = [jax.random.randint(jax.random.fold_in(key, axis), (), 0, length) for axis, length in enumerate(array.shape)]
    longest = array.shape.index(max(array.shape))
    next_to = spot[:longest] + [(spot[longest] + 1) % array.shape[longest]] + spot[longest + 1:]
    return array.at[tuple(spot)].set(least).at[tuple(next_to)].set(top_value)


def shard_levels(key, dims, shards, smallest, largest):
    loudness, own = 1.0, jax.random.fold_in(key, 6)
    for axis_at, parts in shards:
        steps = jnp.exp(jax.random.uniform(jax.random.fold_in(own, axis_at), (parts,), jnp.float32, smallest / len(shards), largest / len(shards)))
        loudness = loudness * jnp.repeat(steps, dims[axis_at] // parts).reshape([-1 if axis == axis_at else 1 for axis in range(len(dims))])
    return loudness


def bell_draw(key, dims, deviation, limit, cuts=(), kind=jnp.bfloat16):
    result = deviation * jax.random.normal(key, dims, jnp.float32)
    if cuts:
        result = result * shard_levels(key, dims, cuts, -0.22, 0.18)
    return jnp.clip(result, -limit, limit).astype(kind)


def setup_inputs(seed: int = 0, part: int = 0) -> dict:
    key_of = jax.random.split(jax.random.key(seed), 5)
    part_keys = jax.random.split(jax.random.fold_in(key_of[4], part), 5)
    return {
        "samples": bell_draw(part_keys[0], (FRAMES, NIN, 2 * NCH), 1.0, 6.0, ((1, 16),)),
        "filter_taps": bell_draw(key_of[1], (TAPS, NCH), TAPS ** -0.5, 2.0, (), jnp.float32),
        "flagged": touch_ends((jax.random.randint(part_keys[2], (NIN,), 0, 16) < 1).astype(jnp.int32), jax.random.fold_in(part_keys[2], 1), 0, 1),
        "input_order": jax.random.permutation(key_of[3], NIN).astype(jnp.int32),
    }


def dft_table(chan_count, chan_window):
    sample_idx = jnp.arange(chan_count, dtype=jnp.int32)
    channel_idx = jnp.arange(chan_window, dtype=jnp.int32)
    phase_step = sample_idx[:, None] * channel_idx[None, :] % chan_count
    phase_angle = phase_step.astype(jnp.float32) * (2.0 * math.pi / chan_count)
    norm_factor = 1.0 / math.sqrt(chan_count)
    cosine_part = jnp.cos(phase_angle) * norm_factor
    sine_part = jnp.sin(phase_angle) * norm_factor
    upper_rows = jnp.concatenate([cosine_part, -sine_part], axis=1)
    lower_rows = jnp.concatenate([sine_part, cosine_part], axis=1)
    return jnp.concatenate([upper_rows, lower_rows], axis=0)

def reference(samples, filter_taps, flagged, input_order):
    tap_weights = jnp.concatenate([filter_taps, filter_taps], axis=1)
    transform_table = dft_table(NCH, CHANS)
    tap_table = (tap_weights[:, :, None] * transform_table[None, :, :]).astype(jnp.bfloat16)
    window_table = tap_table[::-1].astype(jnp.float32).reshape(TAPS * 2 * NCH, 2 * CHANS)
    padded = jnp.concatenate([jnp.zeros((TAPS - 1, NIN, 2 * NCH), jnp.bfloat16), samples], axis=0)

    def one_frame(frame_index):
        window = lax.dynamic_slice_in_dim(padded, frame_index, TAPS, 0).astype(jnp.float32)
        flat_window = jnp.transpose(window, (1, 0, 2)).reshape(NIN, TAPS * 2 * NCH)
        return jnp.dot(flat_window, window_table, precision=lax.Precision.HIGHEST, preferred_element_type=jnp.float32)
    spectra = lax.map(one_frame, jnp.arange(FRAMES, dtype=jnp.int32)).astype(jnp.bfloat16)
    keep_mask = (1 - flagged).astype(jnp.bfloat16)
    used = spectra * keep_mask[None, :, None]
    used = jnp.take(used, input_order, axis=1)
    real_cols = used[:, :, :CHANS]
    imag_cols = used[:, :, CHANS:]

    def one_channel(chan_index):
        real_part = lax.dynamic_index_in_dim(real_cols, chan_index, 2, keepdims=False)
        imag_part = lax.dynamic_index_in_dim(imag_cols, chan_index, 2, keepdims=False)
        real_vis = jnp.dot(real_part.T, real_part, preferred_element_type=jnp.float32) + jnp.dot(imag_part.T, imag_part, preferred_element_type=jnp.float32)
        imag_vis = jnp.dot(imag_part.T, real_part, preferred_element_type=jnp.float32) - jnp.dot(real_part.T, imag_part, preferred_element_type=jnp.float32)
        joined = jnp.concatenate([real_vis, imag_vis], axis=1) * (1.0 / FRAMES)
        return joined.astype(jnp.bfloat16)
    return lax.map(one_channel, jnp.arange(CHANS, dtype=jnp.int32))
```

```python
import functools
import math

import jax
import jax.numpy as jnp
import numpy as np
from jax import lax
from jax.experimental import pallas as pl
from jax.experimental.pallas import tpu as pltpu
from jax.sharding import PartitionSpec as P

LANES = 128
CHUNK_ROWS = 1024
IN_SLOTS = 3
RELAY_LAG = 2
PART_ROWS = 256
VMEM_LIMIT = 48 * 1024 * 1024


def dft_rows(chan_count, sections, chan_dev):
    sample_idx = np.arange(chan_count)
    channel_idx = np.arange(sections * chan_dev)
    angle = (channel_idx[:, None] * sample_idx[None, :] % chan_count) * (2.0 * math.pi / chan_count)
    cosine, sine = np.cos(angle), np.sin(angle)
    real_rows = np.concatenate([cosine, sine], axis=1)
    imag_rows = np.concatenate([-sine, cosine], axis=1)
    rows = np.stack([real_rows, imag_rows], axis=1) / math.sqrt(chan_count)
    return rows.reshape(2 * sections * chan_dev, 2 * chan_count).astype(np.float32)


def filter_kernel(
    chunk_count, sections, samples, taps, dft, gathered,
    inbox, tap_table, terms, wide, outbox, in_sem, send_sem, recv_sem, relay_send, relay_recv,
):
    tap_count, chan_count = taps.shape
    columns = dft.shape[0]
    chunk_frames, nin_loc = inbox.shape[1], inbox.shape[2]
    history = terms.shape[1] - CHUNK_ROWS
    tiles = CHUNK_ROWS // LANES
    me, core = lax.axis_index("tm"), lax.axis_index("inp")

    def fetch(chunk):
        slot = lax.rem(chunk, IN_SLOTS)
        return pltpu.make_async_copy(
            samples.at[pl.ds(chunk * chunk_frames, chunk_frames)], inbox.at[slot], in_sem.at[slot]
        )

    for chunk in range(min(IN_SLOTS, chunk_count)):
        fetch(chunk).start()

    for tap in range(tap_count):
        for half in range(2):
            cols = pl.ds(half * chan_count, chan_count)
            tap_table[pl.ds(tap * columns, columns), cols] = (
                taps[tap : tap + 1, :] * dft[:, cols]
            ).astype(jnp.bfloat16)
    terms[:, :history] = jnp.zeros((terms.shape[0], history), jnp.float32)

    barrier = pltpu.get_barrier_semaphore()

    def greet(step, carry):
        pl.semaphore_signal(
            barrier, inc=1, device_id={"tm": lax.rem(me + step, sections)},
            device_id_type=pl.DeviceIdType.MESH,
        )
        return carry

    lax.fori_loop(1, sections, greet, 0)
    pl.semaphore_signal(
        barrier, inc=1, device_id={"inp": 1 - core}, device_id_type=pl.DeviceIdType.MESH
    )
    pl.semaphore_wait(barrier, sections)

    def message(chunk, step):
        owner = lax.rem(me + step, sections)
        return pltpu.make_async_remote_copy(
            src_ref=outbox.at[chunk, owner],
            dst_ref=gathered.at[core, chunk, me],
            send_sem=send_sem.at[chunk, step],
            recv_sem=recv_sem.at[chunk, me],
            device_id={"tm": owner},
            device_id_type=pl.DeviceIdType.MESH,
        )

    def arrival(chunk, step):
        source = lax.rem(me + step, sections)
        return pltpu.make_async_remote_copy(
            src_ref=outbox.at[chunk, source],
            dst_ref=gathered.at[core, chunk, source],
            send_sem=send_sem.at[chunk, step],
            recv_sem=recv_sem.at[chunk, source],
            device_id={"tm": source},
            device_id_type=pl.DeviceIdType.MESH,
        )

    def relay(chunk, half):
        return pltpu.make_async_remote_copy(
            src_ref=gathered.at[half, chunk],
            dst_ref=gathered.at[half, chunk],
            send_sem=relay_send.at[chunk],
            recv_sem=relay_recv.at[chunk],
            device_id={"inp": 1 - core},
            device_id_type=pl.DeviceIdType.MESH,
        )

    def pass_on(chunk):
        def take(step, carry):
            arrival(chunk, step).wait_recv()
            return carry

        lax.fori_loop(1, sections, take, 0)
        relay(chunk, core).start()

    def one_chunk(chunk, carry):
        fetch(chunk).wait()
        slot = lax.rem(chunk, IN_SLOTS)
        part_frames = PART_ROWS // nin_loc
        for part in range(CHUNK_ROWS // PART_ROWS):
            block = inbox[slot, pl.ds(part * part_frames, part_frames)]
            terms[:, pl.ds(history + part * PART_ROWS, PART_ROWS)] = lax.dot_general(
                tap_table[...], block.reshape(PART_ROWS, 2 * chan_count),
                (((1,), (1,)), ((), ())), preferred_element_type=jnp.float32,
            )

        @pl.when(chunk + IN_SLOTS < chunk_count)
        def _():
            fetch(chunk + IN_SLOTS).start()

        total = None
        for rest in range(0, LANES, nin_loc):
            held = None
            for tap in range(tap_count):
                if tap * nin_loc % LANES != rest:
                    continue
                lead = LANES if rest else 0
                start = history - (tap * nin_loc - rest) - lead
                piece = terms[pl.ds(tap * columns, columns), pl.ds(start, CHUNK_ROWS + lead)]
                held = piece if held is None else held + piece
            if held is None:
                continue
            if rest:
                held = pltpu.roll(held, rest, 1)[:, LANES:]
            total = held if total is None else total + held
        terms[:, :history] = terms[:, CHUNK_ROWS:]
        for tile in range(tiles):
            wide[pl.ds(tile, columns, stride=tiles), :] = total[:, tile * LANES : (tile + 1) * LANES]
        outbox[chunk] = wide[...].astype(jnp.bfloat16).reshape(outbox.shape[1:])
        gathered[core, chunk, me] = outbox[chunk, me]

        def send(step, carry):
            message(chunk, step).start()
            return carry

        lax.fori_loop(1, sections, send, 0)

        @pl.when(chunk >= RELAY_LAG)
        def _():
            pass_on(chunk - RELAY_LAG)

        return carry

    lax.fori_loop(0, chunk_count, one_chunk, 0)

    def late(chunk, carry):
        pass_on(chunk)
        return carry

    lax.fori_loop(max(chunk_count - RELAY_LAG, 0), chunk_count, late, 0)

    def finish(chunk, carry):
        def sent(step, inner):
            message(chunk, step).wait_send()
            return inner

        lax.fori_loop(1, sections, sent, 0)
        relay(chunk, core).wait_send()
        relay(chunk, 1 - core).wait_recv()
        return carry

    lax.fori_loop(0, chunk_count, finish, 0)


def correlate_kernel(
    frames_total, nin_loc, gathered, flagged, order, out, onehot, turned, plain, result, out_sem
):
    chunk_count = gathered.shape[1]
    chan_dev, nin_dev, width = out.shape
    nin_total = width // 2
    pack = LANES // nin_loc
    half_rows = gathered.shape[3] // chan_dev
    depth = pack * chunk_count * half_rows
    first = pl.multiple_of(lax.axis_index("inp") * nin_dev, LANES)
    keep = (1 - flagged[...]).astype(jnp.float32).astype(jnp.bfloat16)
    step = 256
    for base in range(0, nin_total, step):
        index = lax.broadcasted_iota(jnp.int32, (step, nin_total), 0) + base
        onehot[pl.ds(base, step), :] = jnp.where(order[...] == index, 1.0, 0.0).astype(jnp.bfloat16)

    copies = []
    for chan in range(chan_dev):
        rows = pl.ds(chan * half_rows, half_rows)
        groups = []
        for lane in range(pack):
            blocks = []
            for block in range(nin_total // LANES):
                pieces = []
                for source in range(block * pack, (block + 1) * pack):
                    piece = gathered[source % 2, :, source // 2, rows, :]
                    piece = piece.reshape(chunk_count * half_rows, LANES)
                    pieces.append(piece[:, lane * nin_loc : (lane + 1) * nin_loc])
                blocks.append(jnp.concatenate(pieces, axis=1))
            groups.append(jnp.concatenate(blocks, axis=1))
        inputs = jnp.concatenate(groups, axis=0) * keep
        placed = jnp.dot(inputs, onehot[...], preferred_element_type=jnp.float32)
        plain[chan] = placed.astype(jnp.bfloat16)
        split = placed.reshape(depth // half_rows, 2, half_rows // 2, nin_total)
        swapped = jnp.stack([split[:, 1], -split[:, 0]], axis=1)
        turned[chan] = swapped.reshape(depth, nin_total).astype(jnp.bfloat16)
        for part, source in enumerate((plain, turned)):
            product = lax.dot_general(
                source[chan, :, pl.ds(first, nin_dev)], plain[chan],
                (((0,), (0,)), ((), ())), preferred_element_type=jnp.float32,
            )
            columns = pl.ds(part * nin_total, nin_total)
            result[chan, :, columns] = (product * (1.0 / frames_total)).astype(jnp.bfloat16)
            copy = pltpu.make_async_copy(
                result.at[chan, :, columns], out.at[chan, :, columns], out_sem.at[chan, part]
            )
            copy.start()
            copies.append(copy)
    for copy in copies:
        copy.wait()


def shards(chan_dev, sections, samples, filter_taps, flagged, input_order):
    frames_total, nin_loc, width = samples.shape
    tap_count, chan_count = filter_taps.shape
    nin_total = input_order.shape[0]
    columns = 2 * sections * chan_dev
    chunk_frames = CHUNK_ROWS // nin_loc
    chunk_count = frames_total // chunk_frames
    tiles = CHUNK_ROWS // LANES
    history = -(-(tap_count - 1) * nin_loc // LANES) * LANES
    rows = 2 * chan_dev * tiles
    vmem = pl.BlockSpec(memory_space=pltpu.VMEM)
    hbm = pl.BlockSpec(memory_space=pl.ANY)

    gathered = pl.pallas_call(
        functools.partial(filter_kernel, chunk_count, sections),
        out_shape=jax.ShapeDtypeStruct((2, chunk_count, sections, rows, LANES), jnp.bfloat16),
        in_specs=[hbm, vmem, vmem],
        out_specs=vmem,
        scratch_shapes=[
            pltpu.VMEM((IN_SLOTS, chunk_frames, nin_loc, width), jnp.bfloat16),
            pltpu.VMEM((tap_count * columns, width), jnp.bfloat16),
            pltpu.VMEM((tap_count * columns, history + CHUNK_ROWS), jnp.float32),
            pltpu.VMEM((columns * tiles, LANES), jnp.float32),
            pltpu.VMEM((chunk_count, sections, rows, LANES), jnp.bfloat16),
            pltpu.SemaphoreType.DMA((IN_SLOTS,)),
            pltpu.SemaphoreType.DMA((chunk_count, sections)),
            pltpu.SemaphoreType.DMA((chunk_count, sections)),
            pltpu.SemaphoreType.DMA((chunk_count,)),
            pltpu.SemaphoreType.DMA((chunk_count,)),
        ],
        compiler_params=pltpu.CompilerParams(
            collective_id=0, has_side_effects=True, vmem_limit_bytes=VMEM_LIMIT
        ),
        name="filter_exchange",
    )(samples, filter_taps, jnp.asarray(dft_rows(chan_count, sections, chan_dev)))

    nin_dev = nin_total // 2
    depth = 2 * frames_total
    return pl.pallas_call(
        functools.partial(correlate_kernel, frames_total, nin_loc),
        out_shape=jax.ShapeDtypeStruct((chan_dev, nin_dev, 2 * nin_total), jnp.bfloat16),
        in_specs=[vmem, vmem, vmem],
        out_specs=hbm,
        scratch_shapes=[
            pltpu.VMEM((nin_total, nin_total), jnp.bfloat16),
            pltpu.VMEM((chan_dev, depth, nin_total), jnp.bfloat16),
            pltpu.VMEM((chan_dev, depth, nin_total), jnp.bfloat16),
            pltpu.VMEM((chan_dev, nin_dev, 2 * nin_total), jnp.bfloat16),
            pltpu.SemaphoreType.DMA((chan_dev, 2)),
        ],
        compiler_params=pltpu.CompilerParams(vmem_limit_bytes=VMEM_LIMIT),
        name="correlate",
    )(gathered, flagged.reshape(1, nin_total), input_order.reshape(1, nin_total))


def solution(mesh):
    placed = (P("grp", ("tm", "inp"), None), P(), P("grp"), P())
    return jax.shard_map(
        functools.partial(shards, 2, mesh.shape["tm"]),
        mesh=mesh,
        in_specs=placed,
        out_specs=P(("grp", "tm"), "inp", None),
        check_vma=False,
    )
```

```python
import functools
import math

import jax
import jax.numpy as jnp
import numpy as np
from jax import lax
from jax.experimental import pallas as pl
from jax.experimental.pallas import tpu as pltpu
from jax.sharding import PartitionSpec as P

LANES = 128
CHUNK_ROWS = 1024
IN_SLOTS = 3
RELAY_LAG = 4
PART_ROWS = 256
VMEM_LIMIT = 48 * 1024 * 1024


def dft_rows(chan_count, sections, chan_dev):
    sample_idx = np.arange(chan_count)
    channel_idx = np.arange(sections * chan_dev)
    angle = (channel_idx[:, None] * sample_idx[None, :] % chan_count) * (2.0 * math.pi / chan_count)
    cosine, sine = np.cos(angle), np.sin(angle)
    real_rows = np.concatenate([cosine, sine], axis=1)
    imag_rows = np.concatenate([-sine, cosine], axis=1)
    rows = np.stack([real_rows, imag_rows], axis=1) / math.sqrt(chan_count)
    return rows.reshape(2 * sections * chan_dev, 2 * chan_count).astype(np.float32)


def filter_kernel(
    chunk_count, sections, samples, taps_in, dft_in, flagged_in, order_in, plain, turned,
    taps, dft, flagged, order, onehot, gathered, inbox, tap_table, terms, wide, outbox,
    small_sem, in_sem, send_sem, recv_sem, relay_send, relay_recv,
):
    tap_count, chan_count = taps.shape
    columns = dft.shape[0]
    chunk_frames, nin_loc = inbox.shape[1], inbox.shape[2]
    history = terms.shape[1] - CHUNK_ROWS
    tiles = CHUNK_ROWS // LANES
    parts = CHUNK_ROWS // PART_ROWS
    part_frames = PART_ROWS // nin_loc
    nin_total = order.shape[1]
    chan_dev = plain.shape[0]
    pack = LANES // nin_loc
    me, core = lax.axis_index("tm"), lax.axis_index("inp")

    small = [
        pltpu.make_async_copy(source, target, small_sem.at[index])
        for index, (source, target) in enumerate(
            ((taps_in, taps), (dft_in, dft), (flagged_in, flagged), (order_in, order))
        )
    ]
    for copy in small:
        copy.start()

    def fetch(chunk, part):
        slot = lax.rem(chunk, IN_SLOTS)
        return pltpu.make_async_copy(
            samples.at[pl.ds(chunk * chunk_frames + part * part_frames, part_frames)],
            inbox.at[slot, pl.ds(part * part_frames, part_frames)],
            in_sem.at[slot, part],
        )

    for chunk in range(min(IN_SLOTS, chunk_count)):
        for part in range(parts):
            fetch(chunk, part).start()

    barrier = pltpu.get_barrier_semaphore()

    def greet(step, carry):
        pl.semaphore_signal(
            barrier, inc=1, device_id={"tm": lax.rem(me + step, sections)},
            device_id_type=pl.DeviceIdType.MESH,
        )
        return carry

    lax.fori_loop(1, sections, greet, 0)
    pl.semaphore_signal(
        barrier, inc=1, device_id={"inp": 1 - core}, device_id_type=pl.DeviceIdType.MESH
    )

    for copy in small:
        copy.wait()
    for tap in range(tap_count):
        for half in range(2):
            cols = pl.ds(half * chan_count, chan_count)
            tap_table[pl.ds(tap * columns, columns), cols] = (
                taps[tap : tap + 1, :] * dft[:, cols]
            ).astype(jnp.bfloat16)
    terms[:, :history] = jnp.zeros((terms.shape[0], history), jnp.float32)

    def mark(base, carry):
        start = pl.multiple_of(base * PART_ROWS, PART_ROWS)
        index = lax.broadcasted_iota(jnp.int32, (PART_ROWS, nin_total), 0) + start
        onehot[pl.ds(start, PART_ROWS), :] = jnp.where(order[...] == index, 1.0, 0.0).astype(
            jnp.bfloat16
        )
        return carry

    def message(chunk, step):
        owner = lax.rem(me + step, sections)
        return pltpu.make_async_remote_copy(
            src_ref=outbox.at[chunk, owner],
            dst_ref=gathered.at[core, chunk, me],
            send_sem=send_sem.at[chunk, step],
            recv_sem=recv_sem.at[chunk, me],
            device_id={"tm": owner},
            device_id_type=pl.DeviceIdType.MESH,
        )

    def arrival(chunk, step):
        source = lax.rem(me + step, sections)
        return pltpu.make_async_remote_copy(
            src_ref=outbox.at[chunk, source],
            dst_ref=gathered.at[core, chunk, source],
            send_sem=send_sem.at[chunk, step],
            recv_sem=recv_sem.at[chunk, source],
            device_id={"tm": source},
            device_id_type=pl.DeviceIdType.MESH,
        )

    def relay(chunk, half):
        return pltpu.make_async_remote_copy(
            src_ref=gathered.at[half, chunk],
            dst_ref=gathered.at[half, chunk],
            send_sem=relay_send.at[chunk],
            recv_sem=relay_recv.at[chunk],
            device_id={"inp": 1 - core},
            device_id_type=pl.DeviceIdType.MESH,
        )

    def pass_on(chunk):
        def take(step, carry):
            arrival(chunk, step).wait_recv()
            return carry

        lax.fori_loop(1, sections, take, 0)
        relay(chunk, core).start()

    def one_chunk(chunk, carry):
        slot = lax.rem(chunk, IN_SLOTS)
        for part in range(parts):
            fetch(chunk, part).wait()
            block = inbox[slot, pl.ds(part * part_frames, part_frames)]
            terms[:, pl.ds(history + part * PART_ROWS, PART_ROWS)] = lax.dot_general(
                tap_table[...], block.reshape(PART_ROWS, 2 * chan_count),
                (((1,), (1,)), ((), ())), preferred_element_type=jnp.float32,
            )

        @pl.when(chunk + IN_SLOTS < chunk_count)
        def _():
            for part in range(parts):
                fetch(chunk + IN_SLOTS, part).start()

        total = None
        for rest in range(0, LANES, nin_loc):
            held = None
            for tap in range(tap_count):
                if tap * nin_loc % LANES != rest:
                    continue
                lead = LANES if rest else 0
                start = history - (tap * nin_loc - rest) - lead
                piece = terms[pl.ds(tap * columns, columns), pl.ds(start, CHUNK_ROWS + lead)]
                held = piece if held is None else held + piece
            if held is None:
                continue
            if rest:
                held = pltpu.roll(held, rest, 1)[:, LANES:]
            total = held if total is None else total + held
        terms[:, :history] = terms[:, CHUNK_ROWS:]
        for tile in range(tiles):
            wide[pl.ds(tile, columns, stride=tiles), :] = total[:, tile * LANES : (tile + 1) * LANES]
        outbox[chunk] = wide[...].astype(jnp.bfloat16).reshape(outbox.shape[1:])
        gathered[core, chunk, me] = outbox[chunk, me]

        @pl.when(chunk == 0)
        def _():
            lax.fori_loop(0, nin_total // PART_ROWS, mark, 0)
            pl.semaphore_wait(barrier, sections)

        def send(step, carry):
            message(chunk, step).start()
            return carry

        lax.fori_loop(1, sections, send, 0)

        @pl.when(chunk >= RELAY_LAG)
        def _():
            pass_on(chunk - RELAY_LAG)

        return carry

    lax.fori_loop(0, chunk_count, one_chunk, 0)

    keep = (1 - flagged[...]).astype(jnp.float32).astype(jnp.bfloat16)
    batch = max(chunk_count // 2, 1)
    half_rows = gathered.shape[3] // chan_dev
    batch_rows = pack * batch * half_rows

    def place(begin):
        for chunk in range(begin, begin + batch):
            relay(chunk, 1 - core).wait_recv()
        groups = []
        for lane in range(pack):
            blocks = []
            for block in range(nin_total // LANES):
                pieces = []
                for source in range(block * pack, (block + 1) * pack):
                    piece = gathered[source % 2, begin : begin + batch, source // 2]
                    piece = piece.reshape(batch * chan_dev * half_rows, LANES)
                    pieces.append(piece[:, lane * nin_loc : (lane + 1) * nin_loc])
                blocks.append(jnp.concatenate(pieces, axis=1))
            groups.append(jnp.concatenate(blocks, axis=1))
        inputs = jnp.concatenate(groups, axis=0) * keep
        placed = jnp.dot(inputs, onehot[...], preferred_element_type=jnp.float32)
        split = placed.reshape(pack * batch, chan_dev, 2, half_rows // 2, nin_total)
        swapped = jnp.stack([split[:, :, 1], -split[:, :, 0]], axis=2)
        rows = pl.ds(begin // batch * batch_rows, batch_rows)
        for chan in range(chan_dev):
            plain[chan, rows, :] = (
                split[:, chan].reshape(batch_rows, nin_total).astype(jnp.bfloat16)
            )
            turned[chan, rows, :] = (
                swapped[:, chan].reshape(batch_rows, nin_total).astype(jnp.bfloat16)
            )

    late = range(max(chunk_count - RELAY_LAG, 0), chunk_count)
    for chunk in late[: len(late) // 2]:
        pass_on(chunk)
    place(0)
    for chunk in late[len(late) // 2 :]:
        pass_on(chunk)
    for begin in range(batch, chunk_count, batch):
        place(begin)

    def finish(chunk, carry):
        def sent(step, inner):
            message(chunk, step).wait_send()
            return inner

        lax.fori_loop(1, sections, sent, 0)
        relay(chunk, core).wait_send()
        return carry

    lax.fori_loop(0, chunk_count, finish, 0)


def correlate_kernel(frames_total, plain, turned, out, result, out_sem):
    chan_dev, nin_dev, width = out.shape
    nin_total = width // 2
    first = pl.multiple_of(lax.axis_index("inp") * nin_dev, LANES)
    copies = []
    for chan in range(chan_dev):
        for part, source in enumerate((plain, turned)):
            product = lax.dot_general(
                source[chan, :, pl.ds(first, nin_dev)], plain[chan],
                (((0,), (0,)), ((), ())), preferred_element_type=jnp.float32,
            )
            columns = pl.ds(part * nin_total, nin_total)
            result[chan, :, columns] = (product * (1.0 / frames_total)).astype(jnp.bfloat16)
            copy = pltpu.make_async_copy(
                result.at[chan, :, columns], out.at[chan, :, columns], out_sem.at[chan, part]
            )
            copy.start()
            copies.append(copy)
    for copy in copies:
        copy.wait()


def shards(chan_dev, sections, samples, filter_taps, flagged, input_order):
    frames_total, nin_loc, width = samples.shape
    tap_count, chan_count = filter_taps.shape
    nin_total = input_order.shape[0]
    columns = 2 * sections * chan_dev
    chunk_frames = CHUNK_ROWS // nin_loc
    chunk_count = frames_total // chunk_frames
    tiles = CHUNK_ROWS // LANES
    history = -(-(tap_count - 1) * nin_loc // LANES) * LANES
    rows = 2 * chan_dev * tiles
    vmem = pl.BlockSpec(memory_space=pltpu.VMEM)

    hbm = pl.BlockSpec(memory_space=pltpu.HBM)
    nin_dev = nin_total // 2
    depth = 2 * frames_total
    placed = jax.ShapeDtypeStruct((chan_dev, depth, nin_total), jnp.bfloat16)

    plain, turned = pl.pallas_call(
        functools.partial(filter_kernel, chunk_count, sections),
        out_shape=(placed, placed),
        in_specs=[hbm] * 5,
        out_specs=(vmem, vmem),
        scratch_shapes=[
            pltpu.VMEM((tap_count, chan_count), jnp.float32),
            pltpu.VMEM((columns, width), jnp.float32),
            pltpu.VMEM((1, nin_total), jnp.int32),
            pltpu.VMEM((1, nin_total), jnp.int32),
            pltpu.VMEM((nin_total, nin_total), jnp.bfloat16),
            pltpu.VMEM((2, chunk_count, sections, rows, LANES), jnp.bfloat16),
            pltpu.VMEM((IN_SLOTS, chunk_frames, nin_loc, width), jnp.bfloat16),
            pltpu.VMEM((tap_count * columns, width), jnp.bfloat16),
            pltpu.VMEM((tap_count * columns, history + CHUNK_ROWS), jnp.float32),
            pltpu.VMEM((columns * tiles, LANES), jnp.float32),
            pltpu.VMEM((chunk_count, sections, rows, LANES), jnp.bfloat16),
            pltpu.SemaphoreType.DMA((4,)),
            pltpu.SemaphoreType.DMA((IN_SLOTS, CHUNK_ROWS // PART_ROWS)),
            pltpu.SemaphoreType.DMA((chunk_count, sections)),
            pltpu.SemaphoreType.DMA((chunk_count, sections)),
            pltpu.SemaphoreType.DMA((chunk_count,)),
            pltpu.SemaphoreType.DMA((chunk_count,)),
        ],
        compiler_params=pltpu.CompilerParams(
            collective_id=0, has_side_effects=True, vmem_limit_bytes=VMEM_LIMIT
        ),
        name="filter_exchange",
    )(
        samples,
        *(
            pltpu.with_memory_space_constraint(operand, pltpu.HBM)
            for operand in (
                filter_taps, jnp.asarray(dft_rows(chan_count, sections, chan_dev)),
                flagged.reshape(1, nin_total), input_order.reshape(1, nin_total),
            )
        ),
    )

    return pl.pallas_call(
        functools.partial(correlate_kernel, frames_total),
        out_shape=jax.ShapeDtypeStruct((chan_dev, nin_dev, 2 * nin_total), jnp.bfloat16),
        in_specs=[vmem, vmem],
        out_specs=hbm,
        scratch_shapes=[
            pltpu.VMEM((chan_dev, nin_dev, 2 * nin_total), jnp.bfloat16),
            pltpu.SemaphoreType.DMA((chan_dev, 2)),
        ],
        compiler_params=pltpu.CompilerParams(vmem_limit_bytes=VMEM_LIMIT),
        name="correlate",
    )(plain, turned)


def solution(mesh):
    placed = (P("grp", ("tm", "inp"), None), P(), P("grp"), P())
    return jax.shard_map(
        functools.partial(shards, 2, mesh.shape["tm"]),
        mesh=mesh,
        in_specs=placed,
        out_specs=P(("grp", "tm"), "inp", None),
        check_vma=False,
    )
```

```python
import functools
import math

import jax
import jax.numpy as jnp
import numpy as np
from jax import lax
from jax.experimental import pallas as pl
from jax.experimental.pallas import tpu as pltpu
from jax.sharding import PartitionSpec as P

LANES = 128
CHUNK_ROWS = 1024
IN_SLOTS = 3
RELAY_LAG = 4
PART_ROWS = 1024
VMEM_LIMIT = 48 * 1024 * 1024


def dft_rows(chan_count, sections, chan_dev):
    sample_idx = np.arange(chan_count)
    channel_idx = np.arange(sections * chan_dev)
    angle = (channel_idx[:, None] * sample_idx[None, :] % chan_count) * (2.0 * math.pi / chan_count)
    cosine, sine = np.cos(angle), np.sin(angle)
    real_rows = np.concatenate([cosine, sine], axis=1)
    imag_rows = np.concatenate([-sine, cosine], axis=1)
    rows = np.stack([real_rows, imag_rows], axis=1) / math.sqrt(chan_count)
    return rows.reshape(2 * sections * chan_dev, 2 * chan_count).astype(np.float32)


def filter_kernel(
    chunk_count, sections, samples, taps_in, dft_in, flagged_in, order_in, plain, turned,
    taps, dft, flagged, order, onehot, gathered, inbox, tap_table, terms, wide, outbox,
    small_sem, in_sem, send_sem, recv_sem, relay_send, relay_recv,
):
    tap_count, chan_count = taps.shape
    columns = dft.shape[0]
    chunk_frames, nin_loc = inbox.shape[1], inbox.shape[2]
    history = terms.shape[1] - CHUNK_ROWS
    tiles = CHUNK_ROWS // LANES
    parts = CHUNK_ROWS // PART_ROWS
    part_frames = PART_ROWS // nin_loc
    nin_total = order.shape[1]
    chan_dev = plain.shape[0]
    pack = LANES // nin_loc
    me, core = lax.axis_index("tm"), lax.axis_index("inp")

    small = [
        pltpu.make_async_copy(source, target, small_sem.at[index])
        for index, (source, target) in enumerate(
            ((taps_in, taps), (dft_in, dft), (flagged_in, flagged), (order_in, order))
        )
    ]
    for copy in small:
        copy.start()

    def fetch(chunk, part):
        slot = lax.rem(chunk, IN_SLOTS)
        return pltpu.make_async_copy(
            samples.at[pl.ds(chunk * chunk_frames + part * part_frames, part_frames)],
            inbox.at[slot, pl.ds(part * part_frames, part_frames)],
            in_sem.at[slot, part],
        )

    for chunk in range(min(IN_SLOTS, chunk_count)):
        for part in range(parts):
            fetch(chunk, part).start()

    barrier = pltpu.get_barrier_semaphore()

    def greet(step, carry):
        pl.semaphore_signal(
            barrier, inc=1, device_id={"tm": lax.rem(me + step, sections)},
            device_id_type=pl.DeviceIdType.MESH,
        )
        return carry

    lax.fori_loop(1, sections, greet, 0)
    pl.semaphore_signal(
        barrier, inc=1, device_id={"inp": 1 - core}, device_id_type=pl.DeviceIdType.MESH
    )

    for copy in small:
        copy.wait()
    for tap in range(tap_count):
        for half in range(2):
            cols = pl.ds(half * chan_count, chan_count)
            tap_table[pl.ds(tap * columns, columns), cols] = (
                taps[tap : tap + 1, :] * dft[:, cols]
            ).astype(jnp.bfloat16)
    terms[:, :history] = jnp.zeros((terms.shape[0], history), jnp.float32)

    def mark(base, carry):
        start = pl.multiple_of(base * PART_ROWS, PART_ROWS)
        index = lax.broadcasted_iota(jnp.int32, (PART_ROWS, nin_total), 0) + start
        onehot[pl.ds(start, PART_ROWS), :] = jnp.where(order[...] == index, 1.0, 0.0).astype(
            jnp.bfloat16
        )
        return carry

    def message(chunk, step):
        owner = lax.rem(me + step, sections)
        return pltpu.make_async_remote_copy(
            src_ref=outbox.at[chunk, owner],
            dst_ref=gathered.at[core, chunk, me],
            send_sem=send_sem.at[chunk, step],
            recv_sem=recv_sem.at[chunk, me],
            device_id={"tm": owner},
            device_id_type=pl.DeviceIdType.MESH,
        )

    def arrival(chunk, step):
        source = lax.rem(me + step, sections)
        return pltpu.make_async_remote_copy(
            src_ref=outbox.at[chunk, source],
            dst_ref=gathered.at[core, chunk, source],
            send_sem=send_sem.at[chunk, step],
            recv_sem=recv_sem.at[chunk, source],
            device_id={"tm": source},
            device_id_type=pl.DeviceIdType.MESH,
        )

    def relay(chunk, half):
        return pltpu.make_async_remote_copy(
            src_ref=gathered.at[half, chunk],
            dst_ref=gathered.at[half, chunk],
            send_sem=relay_send.at[chunk],
            recv_sem=relay_recv.at[chunk],
            device_id={"inp": 1 - core},
            device_id_type=pl.DeviceIdType.MESH,
        )

    def pass_on(chunk):
        def take(step, carry):
            arrival(chunk, step).wait_recv()
            return carry

        lax.fori_loop(1, sections, take, 0)
        relay(chunk, core).start()

    def one_chunk(chunk, carry):
        slot = lax.rem(chunk, IN_SLOTS)
        for part in range(parts):
            fetch(chunk, part).wait()
            block = inbox[slot, pl.ds(part * part_frames, part_frames)]
            terms[:, pl.ds(history + part * PART_ROWS, PART_ROWS)] = lax.dot_general(
                tap_table[...], block.reshape(PART_ROWS, 2 * chan_count),
                (((1,), (1,)), ((), ())), preferred_element_type=jnp.float32,
            )

        @pl.when(chunk + IN_SLOTS < chunk_count)
        def _():
            for part in range(parts):
                fetch(chunk + IN_SLOTS, part).start()

        total = None
        for rest in range(0, LANES, nin_loc):
            held = None
            for tap in range(tap_count):
                if tap * nin_loc % LANES != rest:
                    continue
                lead = LANES if rest else 0
                start = history - (tap * nin_loc - rest) - lead
                piece = terms[pl.ds(tap * columns, columns), pl.ds(start, CHUNK_ROWS + lead)]
                held = piece if held is None else held + piece
            if held is None:
                continue
            if rest:
                held = pltpu.roll(held, rest, 1)[:, LANES:]
            total = held if total is None else total + held
        terms[:, :history] = terms[:, CHUNK_ROWS:]
        for tile in range(tiles):
            wide[pl.ds(tile, columns, stride=tiles), :] = total[:, tile * LANES : (tile + 1) * LANES]
        outbox[chunk] = wide[...].astype(jnp.bfloat16).reshape(outbox.shape[1:])
        gathered[core, chunk, me] = outbox[chunk, me]

        @pl.when(chunk == 0)
        def _():
            lax.fori_loop(0, nin_total // PART_ROWS, mark, 0)
            pl.semaphore_wait(barrier, sections)

        def send(step, carry):
            message(chunk, step).start()
            return carry

        lax.fori_loop(1, sections, send, 0)

        @pl.when(chunk >= RELAY_LAG)
        def _():
            pass_on(chunk - RELAY_LAG)

        return carry

    lax.fori_loop(0, chunk_count, one_chunk, 0)

    keep = (1 - flagged[...]).astype(jnp.float32).astype(jnp.bfloat16)
    batch = max(chunk_count // 2, 1)
    half_rows = gathered.shape[3] // chan_dev
    batch_rows = pack * batch * half_rows

    def place(begin):
        for chunk in range(begin, begin + batch):
            relay(chunk, 1 - core).wait_recv()
        groups = []
        for lane in range(pack):
            blocks = []
            for block in range(nin_total // LANES):
                pieces = []
                for source in range(block * pack, (block + 1) * pack):
                    piece = gathered[source % 2, begin : begin + batch, source // 2]
                    piece = piece.reshape(batch * chan_dev * half_rows, LANES)
                    pieces.append(piece[:, lane * nin_loc : (lane + 1) * nin_loc])
                blocks.append(jnp.concatenate(pieces, axis=1))
            groups.append(jnp.concatenate(blocks, axis=1))
        inputs = jnp.concatenate(groups, axis=0) * keep
        placed = jnp.dot(inputs, onehot[...], preferred_element_type=jnp.float32)
        split = placed.reshape(pack * batch, chan_dev, 2, half_rows // 2, nin_total)
        swapped = jnp.stack([split[:, :, 1], -split[:, :, 0]], axis=2)
        rows = pl.ds(begin // batch * batch_rows, batch_rows)
        for chan in range(chan_dev):
            plain[chan, rows, :] = (
                split[:, chan].reshape(batch_rows, nin_total).astype(jnp.bfloat16)
            )
            turned[chan, rows, :] = (
                swapped[:, chan].reshape(batch_rows, nin_total).astype(jnp.bfloat16)
            )

    late = range(max(chunk_count - RELAY_LAG, 0), chunk_count)
    for chunk in late[: len(late) // 2]:
        pass_on(chunk)
    place(0)
    for chunk in late[len(late) // 2 :]:
        pass_on(chunk)
    for begin in range(batch, chunk_count, batch):
        place(begin)

    def finish(chunk, carry):
        def sent(step, inner):
            message(chunk, step).wait_send()
            return inner

        lax.fori_loop(1, sections, sent, 0)
        relay(chunk, core).wait_send()
        return carry

    lax.fori_loop(0, chunk_count, finish, 0)


def correlate_kernel(frames_total, plain, turned, out, result, out_sem):
    chan_dev, nin_dev, width = out.shape
    nin_total = width // 2
    first = pl.multiple_of(lax.axis_index("inp") * nin_dev, LANES)
    copies = []
    for chan in range(chan_dev):
        for part, source in enumerate((plain, turned)):
            product = lax.dot_general(
                source[chan, :, pl.ds(first, nin_dev)], plain[chan],
                (((0,), (0,)), ((), ())), preferred_element_type=jnp.float32,
            )
            columns = pl.ds(part * nin_total, nin_total)
            result[chan, :, columns] = (product * (1.0 / frames_total)).astype(jnp.bfloat16)
            copy = pltpu.make_async_copy(
                result.at[chan, :, columns], out.at[chan, :, columns], out_sem.at[chan, part]
            )
            copy.start()
            copies.append(copy)
    for copy in copies:
        copy.wait()


def shards(chan_dev, sections, samples, filter_taps, flagged, input_order):
    frames_total, nin_loc, width = samples.shape
    tap_count, chan_count = filter_taps.shape
    nin_total = input_order.shape[0]
    columns = 2 * sections * chan_dev
    chunk_frames = CHUNK_ROWS // nin_loc
    chunk_count = frames_total // chunk_frames
    tiles = CHUNK_ROWS // LANES
    history = -(-(tap_count - 1) * nin_loc // LANES) * LANES
    rows = 2 * chan_dev * tiles
    vmem = pl.BlockSpec(memory_space=pltpu.VMEM)

    hbm = pl.BlockSpec(memory_space=pltpu.HBM)
    nin_dev = nin_total // 2
    depth = 2 * frames_total
    placed = jax.ShapeDtypeStruct((chan_dev, depth, nin_total), jnp.bfloat16)

    plain, turned = pl.pallas_call(
        functools.partial(filter_kernel, chunk_count, sections),
        out_shape=(placed, placed),
        in_specs=[hbm] * 5,
        out_specs=(vmem, vmem),
        scratch_shapes=[
            pltpu.VMEM((tap_count, chan_count), jnp.float32),
            pltpu.VMEM((columns, width), jnp.float32),
            pltpu.VMEM((1, nin_total), jnp.int32),
            pltpu.VMEM((1, nin_total), jnp.int32),
            pltpu.VMEM((nin_total, nin_total), jnp.bfloat16),
            pltpu.VMEM((2, chunk_count, sections, rows, LANES), jnp.bfloat16),
            pltpu.VMEM((IN_SLOTS, chunk_frames, nin_loc, width), jnp.bfloat16),
            pltpu.VMEM((tap_count * columns, width), jnp.bfloat16),
            pltpu.VMEM((tap_count * columns, history + CHUNK_ROWS), jnp.float32),
            pltpu.VMEM((columns * tiles, LANES), jnp.float32),
            pltpu.VMEM((chunk_count, sections, rows, LANES), jnp.bfloat16),
            pltpu.SemaphoreType.DMA((4,)),
            pltpu.SemaphoreType.DMA((IN_SLOTS, CHUNK_ROWS // PART_ROWS)),
            pltpu.SemaphoreType.DMA((chunk_count, sections)),
            pltpu.SemaphoreType.DMA((chunk_count, sections)),
            pltpu.SemaphoreType.DMA((chunk_count,)),
            pltpu.SemaphoreType.DMA((chunk_count,)),
        ],
        compiler_params=pltpu.CompilerParams(
            collective_id=0, has_side_effects=True, vmem_limit_bytes=VMEM_LIMIT
        ),
        name="filter_exchange",
    )(
        samples,
        *(
            pltpu.with_memory_space_constraint(operand, pltpu.HBM)
            for operand in (
                filter_taps, jnp.asarray(dft_rows(chan_count, sections, chan_dev)),
                flagged.reshape(1, nin_total), input_order.reshape(1, nin_total),
            )
        ),
    )

    return pl.pallas_call(
        functools.partial(correlate_kernel, frames_total),
        out_shape=jax.ShapeDtypeStruct((chan_dev, nin_dev, 2 * nin_total), jnp.bfloat16),
        in_specs=[vmem, vmem],
        out_specs=hbm,
        scratch_shapes=[
            pltpu.VMEM((chan_dev, nin_dev, 2 * nin_total), jnp.bfloat16),
            pltpu.SemaphoreType.DMA((chan_dev, 2)),
        ],
        compiler_params=pltpu.CompilerParams(vmem_limit_bytes=VMEM_LIMIT),
        name="correlate",
    )(plain, turned)


def solution(mesh):
    placed = (P("grp", ("tm", "inp"), None), P(), P("grp"), P())
    return jax.shard_map(
        functools.partial(shards, 2, mesh.shape["tm"]),
        mesh=mesh,
        in_specs=placed,
        out_specs=P(("grp", "tm"), "inp", None),
        check_vma=False,
    )
```
